32 devices in a mesh: group: 1, wide: 32 (over z, y, x, core).
Axes of the slice: x: 2, y: 2, z: 4, core: 2. Of those that a mesh axis runs over, the one named last changes fastest.
Arguments:
- ssd_x: bfloat16 [2048, 4096], P(('group', 'wide')), may hold values from -6 to 6
- ssd_z: bfloat16 [2048, 4096], P(('group', 'wide')), may hold values from -6 to 6
- ssd_b: bfloat16 [2048, 128], P(('group', 'wide')), may hold values from -2 to 2
- ssd_c: bfloat16 [2048, 128], P(('group', 'wide')), may hold values from -2 to 2
- dt_raw: bfloat16 [2048, 64], P(('group', 'wide')), may hold values from -4 to 4
- dt_bias: float32 [64], replicated, may hold values from -4 to -1
- a_log: float32 [64], replicated, may hold values from -1.5 to 1.5
- d_skip: float32 [64], replicated, may hold values from 0.5 to 1.5
- norm_gain: float32 [4096], replicated, may hold values from 0.1 to 1.9
- cache_state: bfloat16 [64, 64, 64, 128], P(('group', 'wide')), may hold values from -2 to 2
- cache_owner: int32 [64], P('group'), may hold values from 0 to 63
- resid: bfloat16 [2048, 2048], P(('group', 'wide')), may hold values from -3 to 3
- w_out: bfloat16 [4096, 2048], P('wide'), may hold values from -0.09375 to 0.09375
- moe_gain: float32 [2048], replicated, may hold values from 0.1 to 1.9
- expert_ids: int32 [2048, 10], P(('group', 'wide')), may hold values from 0 to 31, all different within a row; in each aligned block of 64 rows (0 to 63, 64 to 127, ...) at most 32 rows name the same one
- route_weight: int32 [2048, 10], P(('group', 'wide')), may hold values from 1 to 1023
- expert_home: int32 [32], replicated, may hold values from 0 to 31, each once
- w_gate: bfloat16 [32, 2048, 384], P('wide'), may hold values from -0.125 to 0.125
- w_up: bfloat16 [32, 2048, 384], P('wide'), may hold values from -0.125 to 0.125
- w_down: bfloat16 [32, 384, 2048], P('wide'), may hold values from -0.3125 to 0.3125
Outputs:
- ssd_out: bfloat16 [2048, 4096], P(('group', 'wide'))
- moe_out: bfloat16 [2048, 2048], P(('group', 'wide'))
The draws below stay inside these ranges and needn't reach their ends.
Inputs may be any that keep to these rules, and one draw needn't show every extreme that they name: `cache_owner`: slot s of cache_state holds a cached prefix state; several requests may continue from the same slot. `expert_ids`: each token names 10 different experts. In each aligned block of 64 tokens (the tokens of one device) no expert is named by more than 32 tokens, and in every draw some expert is named by exactly 32 tokens of some block. `expert_home`: A permutation of the experts.
All inputs are finite; a program needn't handle non-finite values.
Results may differ from the reference program's by a relative error of at most 0.02.
Values may be sent and summed in bfloat16 or wider, within the bound.
A program may use at most 128 MiB of HBM per device.

```python
import math
import jax
import jax.numpy as jnp
import numpy as np
from jax import lax

D = 2048
HEADS = 64
HEAD_DIM = 64
STATE = 128
EXP_HID = 384
TOPK = 10
SEQ = 32
TOK_DEV = 64
REQUESTS = 64
SLOTS = 64
TOKENS = 2048
EXPERTS = 32
CAP = 32
N_WIDE = 32


def with_ends(array, rng, smallest, largest):
    spot = [jax.random.randint(jax.random.fold_in(rng, axis), (), 0, length) for axis, length in enumerate(array.shape)]
    longest = array.shape.index(max(array.shape))
    neighbour = spot[:longest] + [(spot[longest] + 1) % array.shape[longest]] + spot[longest + 1:]
    return array.at[tuple(spot)].set(smallest).at[tuple(neighbour)].set(largest)


def steps_of(key, extent, pieces, least, top_value):
    def one(axis_at, shards_of):
        heights = jax.random.uniform(jax.random.fold_in(jax.random.fold_in(key, 6), axis_at), (shards_of,), jnp.float32, least / len(pieces), top_value / len(pieces))
        return jnp.repeat(jnp.exp(heights), extent[axis_at] // shards_of).reshape((-1,) + (1,) * (len(extent) - axis_at - 1))

    loudness = one(*pieces[0])
    for cut in pieces[1:]:
        loudness = loudness * one(*cut)
    return loudness


def shared_out(rng, own, number, rows, number_of, top, bound, slope):
    order = jax.random.permutation(rng, number_of)
    crowded, ordinary = portions_of(number_of, rows * top, bound, slope, True), portions_of(number_of, rows * top, bound, slope, False)
    places = jnp.arange(number_of)

    def named(lengths, offset_by):
        used = int((lengths > 0).sum())
        fixed = max(1, used // 4)
        moved = fixed + (places - fixed + offset_by * (used - fixed)) % max(1, number_of - fixed)
        return jnp.zeros((number_of,), jnp.int32).at[order[jnp.where(places < fixed, places, moved)]].set(jnp.asarray(lengths, jnp.int32))

    lengths = jnp.where(number % 4 == 0, named(crowded, number // 4), named(ordinary, number - number // 4 - 1))
    mixed = jax.random.permutation(jax.random.fold_in(own, 3), number_of)
    giver, taker = mixed[0:number_of // 2 * 2:2], mixed[1:number_of // 2 * 2:2]
    margin = jnp.minimum(lengths[giver] - 1, bound - lengths[taker]) // 2
    margin = jnp.where((giver == order[0]) | (taker == order[0]) | (lengths[taker] == 0), 0, jnp.maximum(margin, 0))
    moved = jax.random.randint(jax.random.fold_in(own, 4), (number_of // 2,), 0, 1 << 20) % (margin + 1)
    lengths = lengths.at[giver].add(-moved).at[taker].add(moved)
    members = jnp.searchsorted(jnp.cumsum(lengths), jnp.arange(rows * top), side="right").astype(jnp.int32)
    table = members.reshape(top, rows).T
    table = table[jax.random.permutation(jax.random.fold_in(own, 1), rows)]
    offset_by = jax.random.randint(jax.random.fold_in(own, 2), (rows, 1), 0, top)
    return jnp.take_along_axis(table, (jnp.arange(top)[None, :] + offset_by) % top, axis=1)


def portions_of(count, total, most, slope, full):
    loads = [(1 << 20) // math.isqrt(standing ** slope) + 1 for standing in range(1, count + 1)]
    largest = most if full else min(most, max(-(-total // count), total * loads[0] // sum(loads)))
    least = 1 if total - largest >= count - 1 else 0
    holding, rest = [largest] + [least] * (count - 1), total - largest - least * (count - 1)
    while rest > 0:
        movable = [i for i in range(1, count) if holding[i] < largest] or [i for i in range(1, count) if holding[i] < most]
        mass, left = sum([loads[i] for i in movable]), rest
        for i in movable:
            more = min(most - holding[i], max(1, left * loads[i] // mass), rest)
            holding[i] = holding[i] + more
            rest = rest - more
    return np.array(holding)


def noise(stream_key, shape, deviation, most, cuts=(), held_as=jnp.bfloat16):
    loudness = steps_of(stream_key, shape, cuts, -0.22, 0.18) if cuts else 1.0
    values = jax.random.normal(stream_key, shape, jnp.float32) * deviation * loudness
    return jnp.minimum(jnp.maximum(values, -most), most).astype(held_as)


def setup_inputs(seed: int = 0, part: int = 0) -> dict:
    seeds = jax.random.split(jax.random.key(seed), 21)
    part_keys = jax.random.split(jax.random.fold_in(seeds[20], part), 21)
    ssd_x = noise(part_keys[0], (TOKENS, HEADS * HEAD_DIM), 1.0, 6.0, ((0, 32),))
    ssd_z = noise(part_keys[1], (TOKENS, HEADS * HEAD_DIM), 1.0, 6.0, ((0, 32),))
    ssd_b = noise(part_keys[2], (TOKENS, STATE), 0.35, 2.0, ((0, 32),))
    ssd_c = noise(part_keys[3], (TOKENS, STATE), 0.35, 2.0, ((0, 32),))
    dt_raw = noise(part_keys[4], (TOKENS, HEADS), 1.0, 4.0, ((0, 32),))
    dt_bias = jnp.clip(jax.random.uniform(seeds[5], (HEADS,), jnp.float32, -4.0, -1.0), -4.0, -1.0)
    a_log = jnp.clip(jax.random.uniform(seeds[6], (HEADS,), jnp.float32, -1.5, 1.5), -1.5, 1.5)
    d_skip = jnp.clip(jax.random.uniform(seeds[7], (HEADS,), jnp.float32, 0.5, 1.5), 0.5, 1.5)
    norm_gain = jnp.clip(1.0 + 0.18 * jax.random.normal(seeds[8], (HEADS * HEAD_DIM,), jnp.float32), 0.1, 1.9)
    cache_state = noise(part_keys[9], (SLOTS, HEADS, HEAD_DIM, STATE), 0.3, 2.0, ((0, 32),))
    cache_owner = with_ends(jax.random.randint(part_keys[10], (REQUESTS,), 0, SLOTS), jax.random.fold_in(part_keys[10], 1), 0, SLOTS - 1).astype(jnp.int32)
    resid = noise(part_keys[11], (TOKENS, D), 0.5, 3.0, ((0, 32),))
    w_out = noise(seeds[12], (HEADS * HEAD_DIM, D), (HEADS * HEAD_DIM) ** -0.5, 0.09375, ((0, 32),))
    moe_gain = jnp.clip(1.0 + 0.18 * jax.random.normal(seeds[13], (D,), jnp.float32), 0.1, 1.9)
    expert_ids_keys = jax.random.split(jax.random.fold_in(part_keys[14], 1), TOKENS // TOK_DEV)
    expert_ids_turns = jax.random.permutation(jax.random.fold_in(part_keys[14], 3), TOKENS // TOK_DEV)
    expert_ids = jax.vmap(lambda own, number: shared_out(jax.random.fold_in(part_keys[14], 2), own, number, TOK_DEV, EXPERTS, TOPK, CAP, 2))(expert_ids_keys, expert_ids_turns).reshape((TOKENS, TOPK))
    route_weight = with_ends(jax.random.randint(part_keys[15], (TOKENS, TOPK), 1, 1024), jax.random.fold_in(part_keys[15], 1), 1, 1023).astype(jnp.int32)
    expert_home = jax.random.permutation(seeds[16], EXPERTS).astype(jnp.int32)
    w_gate = noise(seeds[17], (EXPERTS, D, EXP_HID), D ** -0.5, 0.125, ((0, 32),))
    w_up = noise(seeds[18], (EXPERTS, D, EXP_HID), D ** -0.5, 0.125, ((0, 32),))
    w_down = noise(seeds[19], (EXPERTS, EXP_HID, D), EXP_HID ** -0.5, 0.3125, ((0, 32),))
    return dict(ssd_x=ssd_x, ssd_z=ssd_z, ssd_b=ssd_b, ssd_c=ssd_c, dt_raw=dt_raw, dt_bias=dt_bias, a_log=a_log, d_skip=d_skip, norm_gain=norm_gain, cache_state=cache_state, cache_owner=cache_owner, resid=resid, w_out=w_out, moe_gain=moe_gain, expert_ids=expert_ids, route_weight=route_weight, expert_home=expert_home, w_gate=w_gate, w_up=w_up, w_down=w_down)


def intra_terms(inputs, step_size, cumulative, b_proj, c_proj, skip_gain):
    scores = jnp.einsum('rtn,rsn->rts', c_proj.astype(jnp.float32), b_proj.astype(jnp.float32))
    length = inputs.shape[1]
    causal = jnp.arange(length)[:, None] >= jnp.arange(length)[None, :]
    cum_heads = jnp.swapaxes(cumulative, 1, 2)
    log_gap = cum_heads[..., :, None] - cum_heads[..., None, :]
    decays = jnp.where(causal, jnp.exp(jnp.where(causal, log_gap, 0.0)), 0.0)
    mixing = scores[:, None] * decays * jnp.swapaxes(step_size, 1, 2)[:, :, None, :]
    mixing = lax.optimization_barrier(mixing.astype(jnp.bfloat16)).astype(jnp.float32)
    wide_in = inputs.astype(jnp.float32)
    result = jnp.einsum('rhts,rshp->rthp', mixing, wide_in) + skip_gain[None, None, :, None] * wide_in
    return result.astype(jnp.bfloat16)

def state_terms(c_proj, cumulative, start_state):
    product = jnp.einsum('rtn,rhpn->rthp', c_proj.astype(jnp.float32), start_state.astype(jnp.float32))
    return (product * jnp.exp(cumulative)[..., None]).astype(jnp.bfloat16)

def expert_mlp(row_set, gate_weight, up_weight, down_weight):
    gate_out = jnp.dot(row_set, gate_weight, preferred_element_type=jnp.float32)
    up_out = jnp.dot(row_set, up_weight, preferred_element_type=jnp.float32)
    hidden = (jax.nn.silu(gate_out) * up_out).astype(jnp.bfloat16)
    return jnp.dot(hidden, down_weight, preferred_element_type=jnp.float32).astype(jnp.bfloat16)

def reference(ssd_x, ssd_z, ssd_b, ssd_c, dt_raw, dt_bias, a_log, d_skip, norm_gain, cache_state, cache_owner, resid, w_out, moe_gain, expert_ids, route_weight, expert_home, w_gate, w_up, w_down):
    inputs = ssd_x.reshape(REQUESTS, SEQ, HEADS, HEAD_DIM)
    step_size = jax.nn.softplus(dt_raw.astype(jnp.float32) + dt_bias).reshape(REQUESTS, SEQ, HEADS)
    cumulative = jnp.cumsum(step_size * -jnp.exp(a_log), axis=1)
    b_proj = ssd_b.reshape(REQUESTS, SEQ, STATE)
    c_proj = ssd_c.reshape(REQUESTS, SEQ, STATE)
    intra = intra_terms(inputs, step_size, cumulative, b_proj, c_proj, d_skip)
    start_state = jnp.take(cache_state, cache_owner, axis=0)
    carried = state_terms(c_proj, cumulative, start_state)
    mixed = (intra.astype(jnp.float32) + carried.astype(jnp.float32)).reshape(TOKENS, HEADS * HEAD_DIM)
    gated = mixed * jax.nn.silu(ssd_z.astype(jnp.float32))
    ssd_out = (gated * lax.rsqrt(lax.optimization_barrier(jnp.mean(gated * gated, axis=-1, keepdims=True)) + 1e-05) * norm_gain).astype(jnp.bfloat16)
    wide_moe = resid.astype(jnp.float32) + jnp.dot(ssd_out, w_out, preferred_element_type=jnp.float32)
    normed = (wide_moe * lax.rsqrt(lax.optimization_barrier(jnp.mean(wide_moe * wide_moe, axis=-1, keepdims=True)) + 1e-05) * moe_gain).astype(jnp.bfloat16)
    weight_f = route_weight.astype(jnp.float32)
    share = weight_f / lax.optimization_barrier(jnp.sum(weight_f, axis=-1, keepdims=True))
    target = jnp.take(expert_home, expert_ids)
    limit = N_WIDE * CAP

    def one_expert(position, total):
        chosen = target == position
        weight_tok = lax.optimization_barrier(jnp.sum(jnp.where(chosen, share, 0.0), axis=-1))
        hit_any = jnp.any(chosen, axis=-1)
        picked = jnp.nonzero(hit_any, size=limit, fill_value=0)[0]
        valid = jnp.arange(limit) < jnp.sum(hit_any.astype(jnp.int32))
        outputs = expert_mlp(jnp.take(normed, picked, axis=0), w_gate[position], w_up[position], w_down[position])
        added = outputs.astype(jnp.float32) * jnp.where(valid, jnp.take(weight_tok, picked), 0.0)[:, None]
        return total.at[picked].add(added)
    total = lax.fori_loop(0, EXPERTS, one_expert, jnp.zeros((TOKENS, D), jnp.float32))
    return (ssd_out, total.astype(jnp.bfloat16))
```

```python
import jax
import jax.numpy as jnp
from jax import lax
from jax.sharding import PartitionSpec as P

SEQ = 32


def intra_terms(inputs, step_size, cumulative, b_proj, c_proj, skip_gain):
    scores = jnp.einsum("rtn,rsn->rts", c_proj, b_proj, preferred_element_type=jnp.float32)
    length = inputs.shape[1]
    causal = jnp.arange(length)[:, None] >= jnp.arange(length)[None, :]
    cum_heads = jnp.swapaxes(cumulative, 1, 2)
    log_gap = cum_heads[..., :, None] - cum_heads[..., None, :]
    decays = jnp.where(causal, jnp.exp(jnp.where(causal, log_gap, 0.0)), 0.0)
    mixing = (scores[:, None] * decays * jnp.swapaxes(step_size, 1, 2)[:, :, None, :]).astype(
        jnp.bfloat16
    )
    result = jnp.einsum("rhts,rshp->rthp", mixing, inputs, preferred_element_type=jnp.float32)
    result = result + skip_gain[None, None, :, None] * inputs.astype(jnp.float32)
    return result.astype(jnp.bfloat16)


def state_terms(c_proj, cumulative, start_state):
    product = jnp.einsum("rtn,rhpn->rthp", c_proj, start_state, preferred_element_type=jnp.float32)
    return (product * jnp.exp(cumulative)[..., None]).astype(jnp.bfloat16)


def expert_mlp(row_set, gate_weight, up_weight, down_weight, share):
    gate_out = jnp.dot(row_set, gate_weight, preferred_element_type=jnp.float32)
    up_out = jnp.dot(row_set, up_weight, preferred_element_type=jnp.float32)
    hidden = (jax.nn.silu(gate_out) * up_out).astype(jnp.bfloat16)
    result = jnp.dot(hidden, down_weight, preferred_element_type=jnp.float32)
    return (result * share[:, None]).astype(jnp.bfloat16)


def head_steps(raw_steps, bias_part, rate_part, requests):
    step_size = jax.nn.softplus(raw_steps.astype(jnp.float32) + bias_part)
    step_size = step_size.reshape(requests, SEQ, step_size.shape[-1])
    return (step_size, jnp.cumsum(step_size * rate_part, axis=1))


def local(
    ssd_x,
    ssd_z,
    ssd_b,
    ssd_c,
    dt_raw,
    dt_bias,
    a_log,
    d_skip,
    norm_gain,
    cache_state,
    cache_owner,
    resid,
    w_out,
    moe_gain,
    expert_ids,
    route_weight,
    expert_home,
    w_gate,
    w_up,
    w_down,
):
    devices = lax.axis_size("wide")
    my_index = lax.axis_index("wide")
    tok_dev = ssd_x.shape[0]
    heads_all = dt_raw.shape[1]
    per_dev = heads_all // devices
    head_dim = ssd_x.shape[1] // heads_all
    state_size = ssd_b.shape[1]
    req_local = tok_dev // SEQ
    rates = -jnp.exp(a_log)
    bias_part = lax.dynamic_slice_in_dim(dt_bias, my_index * per_dev, per_dev)
    rate_part = lax.dynamic_slice_in_dim(rates, my_index * per_dev, per_dev)
    by_heads = lax.all_to_all(cache_state, "wide", split_axis=1, concat_axis=0, tiled=True)
    start_state = jnp.take(by_heads, cache_owner, axis=0)
    requests = cache_owner.shape[0]
    tokens_all = requests * SEQ
    local_step, local_cum = head_steps(dt_raw, dt_bias, rates, req_local)
    intra = intra_terms(
        ssd_x.reshape(req_local, SEQ, heads_all, head_dim),
        local_step,
        local_cum,
        ssd_b.reshape(req_local, SEQ, state_size),
        ssd_c.reshape(req_local, SEQ, state_size),
        d_skip,
    )
    intra = intra.reshape(tok_dev, heads_all * head_dim)
    c_all = lax.all_gather(ssd_c, "wide", axis=0, tiled=True)
    head_raw = lax.all_to_all(dt_raw, "wide", split_axis=1, concat_axis=0, tiled=True)
    step_size, cumulative = head_steps(head_raw, bias_part, rate_part, requests)
    carried_head = state_terms(c_all.reshape(requests, SEQ, state_size), cumulative, start_state)
    carried = lax.all_to_all(
        carried_head.reshape(tokens_all, per_dev * head_dim),
        "wide",
        split_axis=0,
        concat_axis=1,
        tiled=True,
    )
    mixed = intra.astype(jnp.float32) + carried.astype(jnp.float32)
    gated = mixed * jax.nn.silu(ssd_z.astype(jnp.float32))
    ssd_out = (
        gated * lax.rsqrt(jnp.mean(gated * gated, axis=-1, keepdims=True) + 1e-05) * norm_gain
    ).astype(jnp.bfloat16)
    width = resid.shape[1]
    projected = jnp.dot(
        ssd_out,
        lax.all_gather(w_out, "wide", axis=0, tiled=True),
        preferred_element_type=jnp.float32,
    )
    wide_moe = resid.astype(jnp.float32) + projected
    normed = (
        wide_moe
        * lax.rsqrt(jnp.mean(wide_moe * wide_moe, axis=-1, keepdims=True) + 1e-05)
        * moe_gain
    ).astype(jnp.bfloat16)
    tokens = lax.all_gather(normed, "wide", axis=0, tiled=True)
    routes = lax.all_gather(
        jnp.concatenate([expert_ids, route_weight], axis=1), "wide", axis=0, tiled=True
    )
    topk = expert_ids.shape[1]
    ids_all, weight_all = routes[:, :topk], routes[:, topk:].astype(jnp.float32)
    my_expert = jnp.argmax(expert_home == my_index).astype(jnp.int32)
    chosen = jnp.sum(jnp.where(ids_all == my_expert, weight_all, 0.0), axis=-1)
    my_share = chosen / jnp.sum(weight_all, axis=-1)
    outputs = expert_mlp(tokens, w_gate[0], w_up[0], w_down[0], my_share)
    moe_out = lax.psum_scatter(outputs, "wide", scatter_dimension=0, tiled=True)
    return (ssd_out, moe_out)


def solution(mesh):
    in_specs = (
        P(("group", "wide"), None),
        P(("group", "wide"), None),
        P(("group", "wide"), None),
        P(("group", "wide"), None),
        P(("group", "wide"), None),
        P(),
        P(),
        P(),
        P(),
        P(("group", "wide"), None, None, None),
        P("group"),
        P(("group", "wide"), None),
        P("wide", None),
        P(),
        P(("group", "wide"), None),
        P(("group", "wide"), None),
        P(),
        P("wide", None, None),
        P("wide", None, None),
        P("wide", None, None),
    )
    out_specs = (P(("group", "wide"), None), P(("group", "wide"), None))
    return jax.shard_map(local, mesh=mesh, in_specs=in_specs, out_specs=out_specs, check_vma=False)
```

```python
import functools

import jax
import jax.numpy as jnp
from jax import lax
from jax.experimental import pallas as pl
from jax.experimental.pallas import tpu as pltpu
from jax.sharding import PartitionSpec as P

SEQ = 32
LANES = 128
MESH = pl.DeviceIdType.MESH


def intra_terms(inputs, step_size, cumulative, b_proj, c_proj, skip_gain):
    scores = jnp.einsum("rtn,rsn->rts", c_proj, b_proj, preferred_element_type=jnp.float32)
    length = inputs.shape[1]
    causal = jnp.arange(length)[:, None] >= jnp.arange(length)[None, :]
    cum_heads = jnp.swapaxes(cumulative, 1, 2)
    log_gap = cum_heads[..., :, None] - cum_heads[..., None, :]
    decays = jnp.where(causal, jnp.exp(jnp.where(causal, log_gap, 0.0)), 0.0)
    mixing = (scores[:, None] * decays * jnp.swapaxes(step_size, 1, 2)[:, :, None, :]).astype(
        jnp.bfloat16
    )
    result = jnp.einsum("rhts,rshp->rthp", mixing, inputs, preferred_element_type=jnp.float32)
    result = result + skip_gain[None, None, :, None] * inputs.astype(jnp.float32)
    return result.astype(jnp.bfloat16)


def state_terms(c_proj, cumulative, start_state):
    product = jnp.einsum("rtn,rhpn->rthp", c_proj, start_state, preferred_element_type=jnp.float32)
    return (product * jnp.exp(cumulative)[..., None]).astype(jnp.bfloat16)


def place(devices):
    me = lax.axis_index("wide")
    return me // 8, me // 4 % 2, me // 2 % 2, me % 2


def expert_kernel(
    planes,
    devices,
    rows_ref,
    gate_hbm,
    up_hbm,
    down_hbm,
    out_ref,
    tok,
    res,
    from_core,
    from_a1,
    from_b1,
    from_a2,
    from_b2,
    from_z,
    w_in,
    w_down,
    local_sem,
    send_sem,
    recv_sem,
):
    z, y, x, c = place(devices)
    me = lax.axis_index("wide")
    half = rows_ref.shape[0] // 2
    width = down_hbm.shape[1]
    hid = down_hbm.shape[0]
    low, high = pl.ds(0, half), pl.ds(half, half)

    def at(zz, yy, xx, cc):
        return {"wide": ((zz * 2 + yy) * 2 + xx) * 2 + cc}

    to_x, to_y, to_c = at(z, y, 1 - x, c), at(z, 1 - y, x, c), at(z, y, x, 1 - c)
    others = [at(lax.rem(z + k, planes), y, x, c) for k in range(1, planes)]
    loads = [
        pltpu.make_async_copy(gate_hbm, w_in.at[:, pl.ds(0, hid)], local_sem.at[0]),
        pltpu.make_async_copy(up_hbm, w_in.at[:, pl.ds(hid, hid)], local_sem.at[1]),
        pltpu.make_async_copy(down_hbm, w_down, local_sem.at[2]),
    ]
    for load in loads:
        load.start()
    tok[z, c, y, x] = rows_ref[...]

    barrier = pltpu.get_barrier_semaphore()
    for peer in [to_x, to_y, to_c] + others:
        pl.semaphore_signal(barrier, inc=1, device_id=peer, device_id_type=MESH)
    pl.semaphore_wait(barrier, planes + 2)

    started = []

    def send(src, dst, kind, out_slot, in_slot, peer):
        copy = pltpu.make_async_remote_copy(
            src_ref=src,
            dst_ref=dst,
            send_sem=send_sem.at[kind, out_slot],
            recv_sem=recv_sem.at[kind, in_slot],
            device_id=peer,
            device_id_type=MESH,
        )
        copy.start()
        started.append(copy)
        return copy

    def arrived(ref, kind, slot):
        pltpu.make_async_copy(ref, ref, recv_sem.at[kind, slot]).wait()

    for k in range(planes - 1, 0, -1):
        mine = tok.at[z, c, y, x]
        send(mine, mine, 0, k, planes - k, others[k - 1])

    def group(j):
        return lax.rem(z + j, planes)

    def spread_1(j):
        q = group(j)
        if j:
            arrived(tok.at[q, c, y, x], 0, j)
        part = tok.at[q, c, y, x, low]
        send(part, part, 1, j, j, to_x)
        part = tok.at[q, c, y, x, high]
        send(part, part, 2, j, j, to_y)

    def spread_2(j):
        q = group(j)
        arrived(tok.at[q, c, y, 1 - x, low], 1, j)
        part = tok.at[q, c, y, :, low]
        send(part, part, 3, j, j, to_y)
        arrived(tok.at[q, c, 1 - y, x, high], 2, j)
        part = tok.at[q, c, :, x, high]
        send(part, part, 4, j, j, to_x)

    def expert(q, side):
        block = tok[q, side].reshape(8 * half, tok.shape[-1])
        both = jnp.dot(block[:, :width], w_in[...], preferred_element_type=jnp.float32)
        hidden = (jax.nn.silu(both[:, :hid]) * both[:, hid:]).astype(jnp.bfloat16)
        lane = lax.broadcasted_iota(jnp.int32, (1, tok.shape[-1] - width), 1)
        mine = (lane == me) | (lane == me + devices)
        share = jnp.sum(
            jnp.where(mine, block[:, width:].astype(jnp.float32), 0.0), axis=1, keepdims=True
        )
        result = jnp.dot(hidden, w_down[...], preferred_element_type=jnp.float32) * share
        res[q, side] = result.astype(jnp.bfloat16).reshape(2, 2, 2 * half, width)

    def spread_3(j):
        q = group(j)
        arrived(tok.at[q, c, 1 - y, :, low], 3, j)
        arrived(tok.at[q, c, :, 1 - x, high], 4, j)
        part = tok.at[q, c]
        send(part, part, 5, j, j, to_c)
        if j == 0:
            for load in loads:
                load.wait()
        expert(q, c)

    def run(j):
        q = group(j)
        arrived(tok.at[q, 1 - c], 5, j)
        expert(q, 1 - c)
        send(res.at[q, 1 - c], from_core.at[j], 6, j, j, to_c)

    def plus(a, b):
        return (a.astype(jnp.float32) + b.astype(jnp.float32)).astype(jnp.bfloat16)

    def sum_1(j):
        q = group(j)
        arrived(from_core.at[j], 6, j)
        res[q, c] = plus(res[q, c], from_core[j])
        send(res.at[q, c, 1 - y, :, low], from_a1.at[j], 7, j, j, to_y)
        send(res.at[q, c, :, 1 - x, high], from_b1.at[j], 8, j, j, to_x)

    def sum_2(j):
        q = group(j)
        arrived(from_a1.at[j], 7, j)
        res[q, c, y, :, low] = plus(res[q, c, y, :, low], from_a1[j])
        send(res.at[q, c, y, 1 - x, low], from_a2.at[j], 9, j, j, to_x)
        arrived(from_b1.at[j], 8, j)
        res[q, c, :, x, high] = plus(res[q, c, :, x, high], from_b1[j])
        send(res.at[q, c, 1 - y, x, high], from_b2.at[j], 10, j, j, to_y)

    def sum_3(j):
        q = group(j)
        arrived(from_a2.at[j], 9, j)
        res[q, c, y, x, low] = plus(res[q, c, y, x, low], from_a2[j])
        arrived(from_b2.at[j], 10, j)
        res[q, c, y, x, high] = plus(res[q, c, y, x, high], from_b2[j])
        if j:
            send(res.at[q, c, y, x], from_z.at[planes - j], 11, j, planes - j, others[j - 1])

    stages = [spread_1, spread_2, spread_3, run, sum_1, sum_2, sum_3]
    for tick in range(planes + len(stages) - 1):
        for number in reversed(range(len(stages))):
            if 0 <= tick - number < planes:
                stages[number](tick - number)

    total = res[z, c, y, x].astype(jnp.float32)
    for j in range(1, planes):
        arrived(from_z.at[j], 11, j)
        total = total + from_z[j].astype(jnp.float32)
    out_ref[...] = total.astype(out_ref.dtype)
    for copy in started:
        copy.wait_send()


def expert_block(rows, gate_weight, up_weight, down_weight, devices):
    planes = devices // 8
    count, wide = rows.shape
    hid, width = down_weight.shape
    half = count // 2

    def held(*shape):
        return pltpu.VMEM(shape, jnp.bfloat16)

    vmem = pl.BlockSpec(memory_space=pltpu.VMEM)
    hbm = pl.BlockSpec(memory_space=pl.ANY)
    return pl.pallas_call(
        functools.partial(expert_kernel, planes, devices),
        out_shape=jax.ShapeDtypeStruct((count, width), jnp.bfloat16),
        in_specs=[vmem, hbm, hbm, hbm],
        out_specs=vmem,
        scratch_shapes=[
            held(planes, 2, 2, 2, count, wide),
            held(planes, 2, 2, 2, count, width),
            held(planes, 2, 2, count, width),
            held(planes, 2, half, width),
            held(planes, 2, half, width),
            held(planes, half, width),
            held(planes, half, width),
            held(planes, count, width),
            held(width, 2 * hid),
            held(hid, width),
            pltpu.SemaphoreType.DMA((3,)),
            pltpu.SemaphoreType.DMA((12, planes)),
            pltpu.SemaphoreType.DMA((12, planes)),
        ],
        compiler_params=pltpu.CompilerParams(
            collective_id=0, has_side_effects=True, vmem_limit_bytes=60 * 1024 * 1024
        ),
        name="expert_block",
    )(rows, gate_weight, up_weight, down_weight)


def head_steps(raw_steps, bias_part, rate_part, requests):
    step_size = jax.nn.softplus(raw_steps.astype(jnp.float32) + bias_part)
    step_size = step_size.reshape(requests, SEQ, step_size.shape[-1])
    return (step_size, jnp.cumsum(step_size * rate_part, axis=1))


def local(
    ssd_x,
    ssd_z,
    ssd_b,
    ssd_c,
    dt_raw,
    dt_bias,
    a_log,
    d_skip,
    norm_gain,
    cache_state,
    cache_owner,
    resid,
    w_out,
    moe_gain,
    expert_ids,
    route_weight,
    expert_home,
    w_gate,
    w_up,
    w_down,
):
    devices = lax.axis_size("wide")
    my_index = lax.axis_index("wide")
    tok_dev = ssd_x.shape[0]
    heads_all = dt_raw.shape[1]
    per_dev = heads_all // devices
    head_dim = ssd_x.shape[1] // heads_all
    state_size = ssd_b.shape[1]
    req_local = tok_dev // SEQ
    rates = -jnp.exp(a_log)
    bias_part = lax.dynamic_slice_in_dim(dt_bias, my_index * per_dev, per_dev)
    rate_part = lax.dynamic_slice_in_dim(rates, my_index * per_dev, per_dev)
    by_heads = lax.all_to_all(cache_state, "wide", split_axis=1, concat_axis=0, tiled=True)
    start_state = jnp.take(by_heads, cache_owner, axis=0)
    requests = cache_owner.shape[0]
    tokens_all = requests * SEQ
    local_step, local_cum = head_steps(dt_raw, dt_bias, rates, req_local)
    intra = intra_terms(
        ssd_x.reshape(req_local, SEQ, heads_all, head_dim),
        local_step,
        local_cum,
        ssd_b.reshape(req_local, SEQ, state_size),
        ssd_c.reshape(req_local, SEQ, state_size),
        d_skip,
    )
    intra = intra.reshape(tok_dev, heads_all * head_dim)
    c_all = lax.all_gather(ssd_c, "wide", axis=0, tiled=True)
    head_raw = lax.all_to_all(dt_raw, "wide", split_axis=1, concat_axis=0, tiled=True)
    step_size, cumulative = head_steps(head_raw, bias_part, rate_part, requests)
    carried_head = state_terms(c_all.reshape(requests, SEQ, state_size), cumulative, start_state)
    carried = lax.all_to_all(
        carried_head.reshape(tokens_all, per_dev * head_dim),
        "wide",
        split_axis=0,
        concat_axis=1,
        tiled=True,
    )
    mixed = intra.astype(jnp.float32) + carried.astype(jnp.float32)
    gated = mixed * jax.nn.silu(ssd_z.astype(jnp.float32))
    ssd_out = (
        gated * lax.rsqrt(jnp.mean(gated * gated, axis=-1, keepdims=True) + 1e-05) * norm_gain
    ).astype(jnp.bfloat16)
    width = resid.shape[1]
    projected = jnp.dot(
        ssd_out,
        lax.all_gather(w_out, "wide", axis=0, tiled=True),
        preferred_element_type=jnp.float32,
    )
    wide_moe = resid.astype(jnp.float32) + projected
    normed = (
        wide_moe
        * lax.rsqrt(jnp.mean(wide_moe * wide_moe, axis=-1, keepdims=True) + 1e-05)
        * moe_gain
    ).astype(jnp.bfloat16)
    weight_f = route_weight.astype(jnp.float32)
    share = weight_f / jnp.sum(weight_f, axis=-1, keepdims=True)
    lookup = expert_ids[..., None] == jnp.arange(expert_home.shape[0], dtype=jnp.int32)
    target = jnp.sum(jnp.where(lookup, expert_home, 0), axis=-1)
    spread = jnp.sum(
        jnp.where(target[..., None] == jnp.arange(devices, dtype=jnp.int32), share[..., None], 0.0),
        axis=1,
    )
    high = spread.astype(jnp.bfloat16)
    low = (spread - high.astype(jnp.float32)).astype(jnp.bfloat16)
    pad = jnp.zeros((tok_dev, -(2 * devices) % LANES), jnp.bfloat16)
    rows = jnp.concatenate([normed, high, low, pad], axis=1)
    moe_out = expert_block(rows, w_gate[0], w_up[0], w_down[0], devices)
    return (ssd_out, moe_out)


def solution(mesh):
    in_specs = (
        P(("group", "wide"), None),
        P(("group", "wide"), None),
        P(("group", "wide"), None),
        P(("group", "wide"), None),
        P(("group", "wide"), None),
        P(),
        P(),
        P(),
        P(),
        P(("group", "wide"), None, None, None),
        P("group"),
        P(("group", "wide"), None),
        P("wide", None),
        P(),
        P(("group", "wide"), None),
        P(("group", "wide"), None),
        P(),
        P("wide", None, None),
        P("wide", None, None),
        P("wide", None, None),
    )
    out_specs = (P(("group", "wide"), None), P(("group", "wide"), None))
    return jax.shard_map(local, mesh=mesh, in_specs=in_specs, out_specs=out_specs, check_vma=False)
```

```python
import functools

import jax
import jax.numpy as jnp
from jax import lax
from jax.experimental import pallas as pl
from jax.experimental.pallas import tpu as pltpu
from jax.sharding import PartitionSpec as P

SEQ = 32
LANES = 128
MESH = pl.DeviceIdType.MESH


def intra_terms(inputs, step_size, cumulative, b_proj, c_proj, skip_gain):
    scores = jnp.einsum("rtn,rsn->rts", c_proj, b_proj, preferred_element_type=jnp.float32)
    length = inputs.shape[1]
    causal = jnp.arange(length)[:, None] >= jnp.arange(length)[None, :]
    cum_heads = jnp.swapaxes(cumulative, 1, 2)
    log_gap = cum_heads[..., :, None] - cum_heads[..., None, :]
    decays = jnp.where(causal, jnp.exp(jnp.where(causal, log_gap, 0.0)), 0.0)
    mixing = (scores[:, None] * decays * jnp.swapaxes(step_size, 1, 2)[:, :, None, :]).astype(
        jnp.bfloat16
    )
    result = jnp.einsum("rhts,rshp->rthp", mixing, inputs, preferred_element_type=jnp.float32)
    result = result + skip_gain[None, None, :, None] * inputs.astype(jnp.float32)
    return result.astype(jnp.bfloat16)


def state_terms(c_proj, start_state):
    product = jnp.einsum("rtn,rhpn->rthp", c_proj, start_state, preferred_element_type=jnp.float32)
    return product.astype(jnp.bfloat16)


def place(devices):
    me = lax.axis_index("wide")
    return me // 8, me // 4 % 2, me // 2 % 2, me % 2


def expert_kernel(
    planes,
    devices,
    rows_ref,
    gate_hbm,
    up_hbm,
    down_hbm,
    out_ref,
    tok,
    res,
    from_core,
    from_a1,
    from_b1,
    from_a2,
    from_b2,
    from_z,
    w_in,
    w_down,
    local_sem,
    send_sem,
    recv_sem,
):
    z, y, x, c = place(devices)
    me = lax.axis_index("wide")
    half = rows_ref.shape[0] // 2
    width = down_hbm.shape[1]
    hid = down_hbm.shape[0]
    low, high = pl.ds(0, half), pl.ds(half, half)

    def at(zz, yy, xx, cc):
        return {"wide": ((zz * 2 + yy) * 2 + xx) * 2 + cc}

    to_x, to_y, to_c = at(z, y, 1 - x, c), at(z, 1 - y, x, c), at(z, y, x, 1 - c)
    others = [at(lax.rem(z + k, planes), y, x, c) for k in range(1, planes)]
    loads = [
        pltpu.make_async_copy(gate_hbm, w_in.at[:, pl.ds(0, hid)], local_sem.at[0]),
        pltpu.make_async_copy(up_hbm, w_in.at[:, pl.ds(hid, hid)], local_sem.at[1]),
        pltpu.make_async_copy(down_hbm, w_down, local_sem.at[2]),
    ]
    for load in loads:
        load.start()
    tok[z, c, y, x] = rows_ref[...]

    barrier = pltpu.get_barrier_semaphore()
    for peer in [to_x, to_y, to_c] + others:
        pl.semaphore_signal(barrier, inc=1, device_id=peer, device_id_type=MESH)
    pl.semaphore_wait(barrier, planes + 2)

    started = []

    def send(src, dst, kind, out_slot, in_slot, peer):
        copy = pltpu.make_async_remote_copy(
            src_ref=src,
            dst_ref=dst,
            send_sem=send_sem.at[kind, out_slot],
            recv_sem=recv_sem.at[kind, in_slot],
            device_id=peer,
            device_id_type=MESH,
        )
        copy.start()
        started.append(copy)
        return copy

    def arrived(ref, kind, slot):
        pltpu.make_async_copy(ref, ref, recv_sem.at[kind, slot]).wait()

    for k in range(planes - 1, 0, -1):
        mine = tok.at[z, c, y, x]
        send(mine, mine, 0, k, planes - k, others[k - 1])

    def group(j):
        return lax.rem(z + j, planes)

    def spread_1(j):
        q = group(j)
        if j:
            arrived(tok.at[q, c, y, x], 0, j)
        part = tok.at[q, c, y, x, low]
        send(part, part, 1, j, j, to_x)
        part = tok.at[q, c, y, x, high]
        send(part, part, 2, j, j, to_y)

    def spread_2(j):
        q = group(j)
        arrived(tok.at[q, c, y, 1 - x, low], 1, j)
        part = tok.at[q, c, y, :, low]
        send(part, part, 3, j, j, to_y)
        arrived(tok.at[q, c, 1 - y, x, high], 2, j)
        part = tok.at[q, c, :, x, high]
        send(part, part, 4, j, j, to_x)

    def expert(q, side):
        block = tok[q, side].reshape(8 * half, tok.shape[-1])
        both = jnp.dot(block[:, :width], w_in[...], preferred_element_type=jnp.float32)
        hidden = (jax.nn.silu(both[:, :hid]) * both[:, hid:]).astype(jnp.bfloat16)
        lane = lax.broadcasted_iota(jnp.int32, (1, tok.shape[-1] - width), 1)
        mine = (lane == me) | (lane == me + devices)
        share = jnp.sum(
            jnp.where(mine, block[:, width:].astype(jnp.float32), 0.0), axis=1, keepdims=True
        )
        result = jnp.dot(hidden, w_down[...], preferred_element_type=jnp.float32) * share
        res[q, side] = result.astype(jnp.bfloat16).reshape(2, 2, 2 * half, width)

    def spread_3(j):
        q = group(j)
        arrived(tok.at[q, c, 1 - y, :, low], 3, j)
        arrived(tok.at[q, c, :, 1 - x, high], 4, j)
        part = tok.at[q, c]
        send(part, part, 5, j, j, to_c)
        if j == 0:
            for load in loads:
                load.wait()
        expert(q, c)

    def run(j):
        q = group(j)
        arrived(tok.at[q, 1 - c], 5, j)
        expert(q, 1 - c)
        send(res.at[q, 1 - c], from_core.at[j], 6, j, j, to_c)

    def plus(a, b):
        return (a.astype(jnp.float32) + b.astype(jnp.float32)).astype(jnp.bfloat16)

    def sum_1(j):
        q = group(j)
        arrived(from_core.at[j], 6, j)
        res[q, c] = plus(res[q, c], from_core[j])
        send(res.at[q, c, 1 - y, :, low], from_a1.at[j], 7, j, j, to_y)
        send(res.at[q, c, :, 1 - x, high], from_b1.at[j], 8, j, j, to_x)

    def sum_2(j):
        q = group(j)
        arrived(from_a1.at[j], 7, j)
        res[q, c, y, :, low] = plus(res[q, c, y, :, low], from_a1[j])
        send(res.at[q, c, y, 1 - x, low], from_a2.at[j], 9, j, j, to_x)
        arrived(from_b1.at[j], 8, j)
        res[q, c, :, x, high] = plus(res[q, c, :, x, high], from_b1[j])
        send(res.at[q, c, 1 - y, x, high], from_b2.at[j], 10, j, j, to_y)

    def sum_3(j):
        q = group(j)
        arrived(from_a2.at[j], 9, j)
        res[q, c, y, x, low] = plus(res[q, c, y, x, low], from_a2[j])
        arrived(from_b2.at[j], 10, j)
        res[q, c, y, x, high] = plus(res[q, c, y, x, high], from_b2[j])
        if j:
            send(res.at[q, c, y, x], from_z.at[planes - j], 11, j, planes - j, others[j - 1])

    stages = [spread_1, spread_2, spread_3, run, sum_1, sum_2, sum_3]
    for tick in range(planes + len(stages) - 1):
        for number in reversed(range(len(stages))):
            if 0 <= tick - number < planes:
                stages[number](tick - number)

    total = res[z, c, y, x].astype(jnp.float32)
    for j in range(1, planes):
        arrived(from_z.at[j], 11, j)
        total = total + from_z[j].astype(jnp.float32)
    out_ref[...] = total.astype(out_ref.dtype)
    for copy in started:
        copy.wait_send()


def expert_block(rows, gate_weight, up_weight, down_weight, devices):
    planes = devices // 8
    count, wide = rows.shape
    hid, width = down_weight.shape
    half = count // 2

    def held(*shape):
        return pltpu.VMEM(shape, jnp.bfloat16)

    vmem = pl.BlockSpec(memory_space=pltpu.VMEM)
    hbm = pl.BlockSpec(memory_space=pl.ANY)
    return pl.pallas_call(
        functools.partial(expert_kernel, planes, devices),
        out_shape=jax.ShapeDtypeStruct((count, width), jnp.bfloat16),
        in_specs=[vmem, hbm, hbm, hbm],
        out_specs=vmem,
        scratch_shapes=[
            held(planes, 2, 2, 2, count, wide),
            held(planes, 2, 2, 2, count, width),
            held(planes, 2, 2, count, width),
            held(planes, 2, half, width),
            held(planes, 2, half, width),
            held(planes, half, width),
            held(planes, half, width),
            held(planes, count, width),
            held(width, 2 * hid),
            held(hid, width),
            pltpu.SemaphoreType.DMA((3,)),
            pltpu.SemaphoreType.DMA((12, planes)),
            pltpu.SemaphoreType.DMA((12, planes)),
        ],
        compiler_params=pltpu.CompilerParams(
            collective_id=0, has_side_effects=True, vmem_limit_bytes=60 * 1024 * 1024
        ),
        name="expert_block",
    )(rows, gate_weight, up_weight, down_weight)


def project_kernel(
    planes, rows_ref, w_hbm, out_ref, weight, arriving, leaving, returned, load_sem, send_sem, recv_sem
):
    z, y, x, c = place(planes * 8)
    depth = weight.shape[0]
    load = pltpu.make_async_copy(w_hbm, weight, load_sem)
    load.start()

    def at(k):
        return {"wide": ((lax.rem(z + k, planes) * 2 + y) * 2 + x) * 2 + c}

    def columns(k):
        first = lax.rem(z + k, planes) * depth
        return pl.ds(pl.multiple_of(first, depth), depth)

    def send(src, dst, kind, k):
        copy = pltpu.make_async_remote_copy(
            src_ref=src,
            dst_ref=dst.at[planes - k],
            send_sem=send_sem.at[kind, k],
            recv_sem=recv_sem.at[kind, planes - k],
            device_id=at(k),
            device_id_type=MESH,
        )
        copy.start()
        return copy

    def arrived(ref, kind, slot):
        pltpu.make_async_copy(ref, ref, recv_sem.at[kind, slot]).wait()

    barrier = pltpu.get_barrier_semaphore()
    for k in range(1, planes):
        pl.semaphore_signal(barrier, inc=1, device_id=at(k), device_id_type=MESH)
    pl.semaphore_wait(barrier, planes - 1)

    started = []
    for k in range(planes - 1, 0, -1):
        started.append(send(rows_ref.at[:, columns(k)], arriving, 0, k))
    load.wait()
    total = jnp.dot(rows_ref[:, columns(0)], weight[...], preferred_element_type=jnp.float32)
    out_ref[...] = total
    for k in range(1, planes):
        arrived(arriving.at[k], 0, k)
        part = jnp.dot(arriving[k], weight[...], preferred_element_type=jnp.float32)
        leaving[k] = part.astype(leaving.dtype)
        started.append(send(leaving.at[k], returned, 1, k))
    for k in range(1, planes):
        arrived(returned.at[k], 1, k)
        out_ref[...] += returned[k].astype(jnp.float32)
    for copy in started:
        copy.wait_send()


def project_block(rows, weight, devices):
    planes = devices // 8
    count = rows.shape[0]
    depth, width = weight.shape
    return pl.pallas_call(
        functools.partial(project_kernel, planes),
        out_shape=jax.ShapeDtypeStruct((count, width), jnp.float32),
        in_specs=[pl.BlockSpec(memory_space=pltpu.VMEM), pl.BlockSpec(memory_space=pl.ANY)],
        out_specs=pl.BlockSpec(memory_space=pltpu.VMEM),
        scratch_shapes=[
            pltpu.VMEM((depth, width), jnp.bfloat16),
            pltpu.VMEM((planes, count, depth), jnp.bfloat16),
            pltpu.VMEM((planes, count, width), jnp.bfloat16),
            pltpu.VMEM((planes, count, width), jnp.bfloat16),
            pltpu.SemaphoreType.DMA,
            pltpu.SemaphoreType.DMA((2, planes)),
            pltpu.SemaphoreType.DMA((2, planes)),
        ],
        compiler_params=pltpu.CompilerParams(
            collective_id=1, has_side_effects=True, vmem_limit_bytes=40 * 1024 * 1024
        ),
        name="project_block",
    )(rows, weight)


def head_steps(raw_steps, bias_part, rate_part, requests):
    step_size = jax.nn.softplus(raw_steps.astype(jnp.float32) + bias_part)
    step_size = step_size.reshape(requests, SEQ, step_size.shape[-1])
    return (step_size, jnp.cumsum(step_size * rate_part, axis=1))


def local(
    ssd_x,
    ssd_z,
    ssd_b,
    ssd_c,
    dt_raw,
    dt_bias,
    a_log,
    d_skip,
    norm_gain,
    cache_state,
    cache_owner,
    resid,
    w_out,
    moe_gain,
    expert_ids,
    route_weight,
    expert_home,
    w_gate,
    w_up,
    w_down,
):
    devices = lax.axis_size("wide")
    my_index = lax.axis_index("wide")
    tok_dev = ssd_x.shape[0]
    heads_all = dt_raw.shape[1]
    per_dev = heads_all // devices
    head_dim = ssd_x.shape[1] // heads_all
    state_size = ssd_b.shape[1]
    req_local = tok_dev // SEQ
    rates = -jnp.exp(a_log)
    members = [list(range(first, first + 8)) for first in range(0, devices, 8)]
    w_plane = lax.all_gather(w_out, "wide", axis=0, tiled=True, axis_index_groups=members)
    by_heads = lax.all_to_all(cache_state, "wide", split_axis=1, concat_axis=0, tiled=True)
    start_state = jnp.take(by_heads, cache_owner, axis=0)
    requests = cache_owner.shape[0]
    tokens_all = requests * SEQ
    local_step, local_cum = head_steps(dt_raw, dt_bias, rates, req_local)
    intra = intra_terms(
        ssd_x.reshape(req_local, SEQ, heads_all, head_dim),
        local_step,
        local_cum,
        ssd_b.reshape(req_local, SEQ, state_size),
        ssd_c.reshape(req_local, SEQ, state_size),
        d_skip,
    )
    intra = intra.reshape(tok_dev, heads_all * head_dim)
    c_all = lax.all_gather(ssd_c, "wide", axis=0, tiled=True)
    carried_head = state_terms(c_all.reshape(requests, SEQ, state_size), start_state)
    carried = lax.all_to_all(
        carried_head.reshape(tokens_all, per_dev * head_dim),
        "wide",
        split_axis=0,
        concat_axis=1,
        tiled=True,
    )
    decayed = carried.astype(jnp.float32).reshape(req_local, SEQ, heads_all, head_dim)
    decayed = decayed * jnp.exp(local_cum)[..., None]
    mixed = intra.astype(jnp.float32) + decayed.reshape(tok_dev, heads_all * head_dim)
    gated = mixed * jax.nn.silu(ssd_z.astype(jnp.float32))
    ssd_out = (
        gated * lax.rsqrt(jnp.mean(gated * gated, axis=-1, keepdims=True) + 1e-05) * norm_gain
    ).astype(jnp.bfloat16)
    width = resid.shape[1]
    projected = project_block(ssd_out, w_plane, devices)
    wide_moe = resid.astype(jnp.float32) + projected
    normed = (
        wide_moe
        * lax.rsqrt(jnp.mean(wide_moe * wide_moe, axis=-1, keepdims=True) + 1e-05)
        * moe_gain
    ).astype(jnp.bfloat16)
    weight_f = route_weight.astype(jnp.float32)
    share = weight_f / jnp.sum(weight_f, axis=-1, keepdims=True)
    lookup = expert_ids[..., None] == jnp.arange(expert_home.shape[0], dtype=jnp.int32)
    target = jnp.sum(jnp.where(lookup, expert_home, 0), axis=-1)
    spread = jnp.sum(
        jnp.where(target[..., None] == jnp.arange(devices, dtype=jnp.int32), share[..., None], 0.0),
        axis=1,
    )
    high = spread.astype(jnp.bfloat16)
    low = (spread - high.astype(jnp.float32)).astype(jnp.bfloat16)
    pad = jnp.zeros((tok_dev, -(2 * devices) % LANES), jnp.bfloat16)
    rows = jnp.concatenate([normed, high, low, pad], axis=1)
    moe_out = expert_block(rows, w_gate[0], w_up[0], w_down[0], devices)
    return (ssd_out, moe_out)


def solution(mesh):
    in_specs = (
        P(("group", "wide"), None),
        P(("group", "wide"), None),
        P(("group", "wide"), None),
        P(("group", "wide"), None),
        P(("group", "wide"), None),
        P(),
        P(),
        P(),
        P(),
        P(("group", "wide"), None, None, None),
        P("group"),
        P(("group", "wide"), None),
        P("wide", None),
        P(),
        P(("group", "wide"), None),
        P(("group", "wide"), None),
        P(),
        P("wide", None, None),
        P("wide", None, None),
        P("wide", None, None),
    )
    out_specs = (P(("group", "wide"), None), P(("group", "wide"), None))
    return jax.shard_map(local, mesh=mesh, in_specs=in_specs, out_specs=out_specs, check_vma=False)
```

```python
import functools

import jax
import jax.numpy as jnp
from jax import lax
from jax.experimental import pallas as pl
from jax.experimental.pallas import tpu as pltpu
from jax.sharding import PartitionSpec as P

SEQ = 32
LANES = 128
MESH = pl.DeviceIdType.MESH


def intra_terms(inputs, step_size, cumulative, b_proj, c_proj, skip_gain):
    scores = jnp.einsum("rtn,rsn->rts", c_proj, b_proj, preferred_element_type=jnp.float32)
    length = inputs.shape[1]
    causal = jnp.arange(length)[:, None] >= jnp.arange(length)[None, :]
    cum_heads = jnp.swapaxes(cumulative, 1, 2)
    log_gap = cum_heads[..., :, None] - cum_heads[..., None, :]
    decays = jnp.where(causal, jnp.exp(jnp.where(causal, log_gap, 0.0)), 0.0)
    mixing = (scores[:, None] * decays * jnp.swapaxes(step_size, 1, 2)[:, :, None, :]).astype(
        jnp.bfloat16
    )
    result = jnp.einsum("rhts,rshp->rthp", mixing, inputs, preferred_element_type=jnp.float32)
    result = result + skip_gain[None, None, :, None] * inputs.astype(jnp.float32)
    return result.astype(jnp.bfloat16)


def state_terms(c_proj, start_state):
    product = jnp.einsum("rtn,rhpn->rthp", c_proj, start_state, preferred_element_type=jnp.float32)
    return product.astype(jnp.bfloat16)


def place(devices):
    me = lax.axis_index("wide")
    return me // 8, me // 4 % 2, me // 2 % 2, me % 2


def expert_kernel(
    planes,
    devices,
    rows_ref,
    gate_hbm,
    up_hbm,
    down_hbm,
    out_ref,
    tok,
    res,
    from_core,
    from_a1,
    from_b1,
    from_a2,
    from_b2,
    from_z,
    w_in,
    w_down,
    local_sem,
    send_sem,
    recv_sem,
):
    z, y, x, c = place(devices)
    me = lax.axis_index("wide")
    half = rows_ref.shape[0] // 2
    width = down_hbm.shape[1]
    hid = down_hbm.shape[0]
    low, high = pl.ds(0, half), pl.ds(half, half)

    def at(zz, yy, xx, cc):
        return {"wide": ((zz * 2 + yy) * 2 + xx) * 2 + cc}

    to_x, to_y, to_c = at(z, y, 1 - x, c), at(z, 1 - y, x, c), at(z, y, x, 1 - c)
    others = [at(lax.rem(z + k, planes), y, x, c) for k in range(1, planes)]
    loads = [
        pltpu.make_async_copy(gate_hbm, w_in.at[:, pl.ds(0, hid)], local_sem.at[0]),
        pltpu.make_async_copy(up_hbm, w_in.at[:, pl.ds(hid, hid)], local_sem.at[1]),
        pltpu.make_async_copy(down_hbm, w_down, local_sem.at[2]),
    ]
    for load in loads:
        load.start()
    tok[z, c, y, x] = rows_ref[...]

    barrier = pltpu.get_barrier_semaphore()
    for peer in [to_x, to_y, to_c] + others:
        pl.semaphore_signal(barrier, inc=1, device_id=peer, device_id_type=MESH)
    pl.semaphore_wait(barrier, planes + 2)

    started = []

    def send(src, dst, kind, out_slot, in_slot, peer):
        copy = pltpu.make_async_remote_copy(
            src_ref=src,
            dst_ref=dst,
            send_sem=send_sem.at[kind, out_slot],
            recv_sem=recv_sem.at[kind, in_slot],
            device_id=peer,
            device_id_type=MESH,
        )
        copy.start()
        started.append(copy)
        return copy

    def arrived(ref, kind, slot):
        pltpu.make_async_copy(ref, ref, recv_sem.at[kind, slot]).wait()

    for k in range(planes - 1, 0, -1):
        mine = tok.at[z, c, y, x]
        send(mine, mine, 0, k, planes - k, others[k - 1])

    def group(j):
        return lax.rem(z + j, planes)

    def spread_1(j):
        q = group(j)
        if j:
            arrived(tok.at[q, c, y, x], 0, j)
        part = tok.at[q, c, y, x, low]
        send(part, part, 1, j, j, to_x)
        part = tok.at[q, c, y, x, high]
        send(part, part, 2, j, j, to_y)

    def spread_2(j):
        q = group(j)
        arrived(tok.at[q, c, y, 1 - x, low], 1, j)
        part = tok.at[q, c, y, :, low]
        send(part, part, 3, j, j, to_y)
        arrived(tok.at[q, c, 1 - y, x, high], 2, j)
        part = tok.at[q, c, :, x, high]
        send(part, part, 4, j, j, to_x)

    def expert(q, side):
        block = tok[q, side].reshape(8 * half, tok.shape[-1])
        both = jnp.dot(block[:, :width], w_in[...], preferred_element_type=jnp.float32)
        hidden = (jax.nn.silu(both[:, :hid]) * both[:, hid:]).astype(jnp.bfloat16)
        lane = lax.broadcasted_iota(jnp.int32, (1, tok.shape[-1] - width), 1)
        mine = (lane == me) | (lane == me + devices)
        share = jnp.sum(
            jnp.where(mine, block[:, width:].astype(jnp.float32), 0.0), axis=1, keepdims=True
        )
        result = jnp.dot(hidden, w_down[...], preferred_element_type=jnp.float32) * share
        res[q, side] = result.astype(jnp.bfloat16).reshape(2, 2, 2 * half, width)

    def spread_3(j):
        q = group(j)
        arrived(tok.at[q, c, 1 - y, :, low], 3, j)
        arrived(tok.at[q, c, :, 1 - x, high], 4, j)
        part = tok.at[q, c]
        send(part, part, 5, j, j, to_c)
        if j == 0:
            for load in loads:
                load.wait()
        expert(q, c)

    def run(j):
        q = group(j)
        arrived(tok.at[q, 1 - c], 5, j)
        expert(q, 1 - c)
        send(res.at[q, 1 - c], from_core.at[j], 6, j, j, to_c)

    def plus(a, b):
        return (a.astype(jnp.float32) + b.astype(jnp.float32)).astype(jnp.bfloat16)

    def sum_1(j):
        q = group(j)
        arrived(from_core.at[j], 6, j)
        res[q, c] = plus(res[q, c], from_core[j])
        send(res.at[q, c, 1 - y, :, low], from_a1.at[j], 7, j, j, to_y)
        send(res.at[q, c, :, 1 - x, high], from_b1.at[j], 8, j, j, to_x)

    def sum_2(j):
        q = group(j)
        arrived(from_a1.at[j], 7, j)
        res[q, c, y, :, low] = plus(res[q, c, y, :, low], from_a1[j])
        send(res.at[q, c, y, 1 - x, low], from_a2.at[j], 9, j, j, to_x)
        arrived(from_b1.at[j], 8, j)
        res[q, c, :, x, high] = plus(res[q, c, :, x, high], from_b1[j])
        send(res.at[q, c, 1 - y, x, high], from_b2.at[j], 10, j, j, to_y)

    def sum_3(j):
        q = group(j)
        arrived(from_a2.at[j], 9, j)
        res[q, c, y, x, low] = plus(res[q, c, y, x, low], from_a2[j])
        arrived(from_b2.at[j], 10, j)
        res[q, c, y, x, high] = plus(res[q, c, y, x, high], from_b2[j])
        if j:
            send(res.at[q, c, y, x], from_z.at[planes - j], 11, j, planes - j, others[j - 1])

    stages = [spread_1, spread_2, spread_3, run, sum_1, sum_2, sum_3]
    for tick in range(planes + len(stages) - 1):
        for number in (1, 0, 6, 5, 4, 3, 2):
            if 0 <= tick - number < planes:
                stages[number](tick - number)

    total = res[z, c, y, x].astype(jnp.float32)
    for j in range(1, planes):
        arrived(from_z.at[j], 11, j)
        total = total + from_z[j].astype(jnp.float32)
    out_ref[...] = total.astype(out_ref.dtype)
    for copy in started:
        copy.wait_send()


def expert_block(rows, gate_weight, up_weight, down_weight, devices):
    planes = devices // 8
    count, wide = rows.shape
    hid, width = down_weight.shape
    half = count // 2

    def held(*shape):
        return pltpu.VMEM(shape, jnp.bfloat16)

    vmem = pl.BlockSpec(memory_space=pltpu.VMEM)
    hbm = pl.BlockSpec(memory_space=pl.ANY)
    return pl.pallas_call(
        functools.partial(expert_kernel, planes, devices),
        out_shape=jax.ShapeDtypeStruct((count, width), jnp.bfloat16),
        in_specs=[vmem, hbm, hbm, hbm],
        out_specs=vmem,
        scratch_shapes=[
            held(planes, 2, 2, 2, count, wide),
            held(planes, 2, 2, 2, count, width),
            held(planes, 2, 2, count, width),
            held(planes, 2, half, width),
            held(planes, 2, half, width),
            held(planes, half, width),
            held(planes, half, width),
            held(planes, count, width),
            held(width, 2 * hid),
            held(hid, width),
            pltpu.SemaphoreType.DMA((3,)),
            pltpu.SemaphoreType.DMA((12, planes)),
            pltpu.SemaphoreType.DMA((12, planes)),
        ],
        compiler_params=pltpu.CompilerParams(
            collective_id=0, has_side_effects=True, vmem_limit_bytes=60 * 1024 * 1024
        ),
        name="expert_block",
    )(rows, gate_weight, up_weight, down_weight)


def project_kernel(
    planes, rows_ref, w_hbm, out_ref, weight, arriving, leaving, returned, load_sem, send_sem, recv_sem
):
    z, y, x, c = place(planes * 8)
    depth = weight.shape[0]
    load = pltpu.make_async_copy(w_hbm, weight, load_sem)
    load.start()

    def at(k):
        return {"wide": ((lax.rem(z + k, planes) * 2 + y) * 2 + x) * 2 + c}

    def columns(k):
        first = lax.rem(z + k, planes) * depth
        return pl.ds(pl.multiple_of(first, depth), depth)

    def send(src, dst, kind, k):
        copy = pltpu.make_async_remote_copy(
            src_ref=src,
            dst_ref=dst.at[planes - k],
            send_sem=send_sem.at[kind, k],
            recv_sem=recv_sem.at[kind, planes - k],
            device_id=at(k),
            device_id_type=MESH,
        )
        copy.start()
        return copy

    def arrived(ref, kind, slot):
        pltpu.make_async_copy(ref, ref, recv_sem.at[kind, slot]).wait()

    barrier = pltpu.get_barrier_semaphore()
    for k in range(1, planes):
        pl.semaphore_signal(barrier, inc=1, device_id=at(k), device_id_type=MESH)
    pl.semaphore_wait(barrier, planes - 1)

    started = []
    for k in range(planes - 1, 0, -1):
        started.append(send(rows_ref.at[:, columns(k)], arriving, 0, k))
    load.wait()
    total = jnp.dot(rows_ref[:, columns(0)], weight[...], preferred_element_type=jnp.float32)
    out_ref[...] = total
    for k in range(1, planes):
        arrived(arriving.at[k], 0, k)
        part = jnp.dot(arriving[k], weight[...], preferred_element_type=jnp.float32)
        leaving[k] = part.astype(leaving.dtype)
        started.append(send(leaving.at[k], returned, 1, k))
    for k in range(1, planes):
        arrived(returned.at[k], 1, k)
        out_ref[...] += returned[k].astype(jnp.float32)
    for copy in started:
        copy.wait_send()


def project_block(rows, weight, devices):
    planes = devices // 8
    count = rows.shape[0]
    depth, width = weight.shape
    return pl.pallas_call(
        functools.partial(project_kernel, planes),
        out_shape=jax.ShapeDtypeStruct((count, width), jnp.float32),
        in_specs=[pl.BlockSpec(memory_space=pltpu.VMEM), pl.BlockSpec(memory_space=pl.ANY)],
        out_specs=pl.BlockSpec(memory_space=pltpu.VMEM),
        scratch_shapes=[
            pltpu.VMEM((depth, width), jnp.bfloat16),
            pltpu.VMEM((planes, count, depth), jnp.bfloat16),
            pltpu.VMEM((planes, count, width), jnp.bfloat16),
            pltpu.VMEM((planes, count, width), jnp.bfloat16),
            pltpu.SemaphoreType.DMA,
            pltpu.SemaphoreType.DMA((2, planes)),
            pltpu.SemaphoreType.DMA((2, planes)),
        ],
        compiler_params=pltpu.CompilerParams(
            collective_id=1, has_side_effects=True, vmem_limit_bytes=40 * 1024 * 1024
        ),
        name="project_block",
    )(rows, weight)


def head_steps(raw_steps, bias_part, rate_part, requests):
    step_size = jax.nn.softplus(raw_steps.astype(jnp.float32) + bias_part)
    step_size = step_size.reshape(requests, SEQ, step_size.shape[-1])
    return (step_size, jnp.cumsum(step_size * rate_part, axis=1))


def local(
    ssd_x,
    ssd_z,
    ssd_b,
    ssd_c,
    dt_raw,
    dt_bias,
    a_log,
    d_skip,
    norm_gain,
    cache_state,
    cache_owner,
    resid,
    w_out,
    moe_gain,
    expert_ids,
    route_weight,
    expert_home,
    w_gate,
    w_up,
    w_down,
):
    devices = lax.axis_size("wide")
    my_index = lax.axis_index("wide")
    tok_dev = ssd_x.shape[0]
    heads_all = dt_raw.shape[1]
    per_dev = heads_all // devices
    head_dim = ssd_x.shape[1] // heads_all
    state_size = ssd_b.shape[1]
    req_local = tok_dev // SEQ
    rates = -jnp.exp(a_log)
    members = [list(range(first, first + 8)) for first in range(0, devices, 8)]
    by_heads = lax.all_to_all(cache_state, "wide", split_axis=1, concat_axis=0, tiled=True)
    by_heads, w_out = lax.optimization_barrier((by_heads, w_out))
    w_plane = lax.all_gather(w_out, "wide", axis=0, tiled=True, axis_index_groups=members)
    start_state = jnp.take(by_heads, cache_owner, axis=0)
    requests = cache_owner.shape[0]
    tokens_all = requests * SEQ
    local_step, local_cum = head_steps(dt_raw, dt_bias, rates, req_local)
    intra = intra_terms(
        ssd_x.reshape(req_local, SEQ, heads_all, head_dim),
        local_step,
        local_cum,
        ssd_b.reshape(req_local, SEQ, state_size),
        ssd_c.reshape(req_local, SEQ, state_size),
        d_skip,
    )
    intra = intra.reshape(tok_dev, heads_all * head_dim)
    c_all = lax.all_gather(ssd_c, "wide", axis=0, tiled=True)
    carried_head = state_terms(c_all.reshape(requests, SEQ, state_size), start_state)
    carried = lax.all_to_all(
        carried_head.reshape(tokens_all, per_dev * head_dim),
        "wide",
        split_axis=0,
        concat_axis=1,
        tiled=True,
    )
    decayed = carried.astype(jnp.float32).reshape(req_local, SEQ, heads_all, head_dim)
    decayed = decayed * jnp.exp(local_cum)[..., None]
    mixed = intra.astype(jnp.float32) + decayed.reshape(tok_dev, heads_all * head_dim)
    gated = mixed * jax.nn.silu(ssd_z.astype(jnp.float32))
    ssd_out = (
        gated * lax.rsqrt(jnp.mean(gated * gated, axis=-1, keepdims=True) + 1e-05) * norm_gain
    ).astype(jnp.bfloat16)
    width = resid.shape[1]
    projected = project_block(ssd_out, w_plane, devices)
    wide_moe = resid.astype(jnp.float32) + projected
    normed = (
        wide_moe
        * lax.rsqrt(jnp.mean(wide_moe * wide_moe, axis=-1, keepdims=True) + 1e-05)
        * moe_gain
    ).astype(jnp.bfloat16)
    weight_f = route_weight.astype(jnp.float32)
    share = weight_f / jnp.sum(weight_f, axis=-1, keepdims=True)
    lookup = expert_ids[..., None] == jnp.arange(expert_home.shape[0], dtype=jnp.int32)
    target = jnp.sum(jnp.where(lookup, expert_home, 0), axis=-1)
    spread = jnp.sum(
        jnp.where(target[..., None] == jnp.arange(devices, dtype=jnp.int32), share[..., None], 0.0),
        axis=1,
    )
    high = spread.astype(jnp.bfloat16)
    low = (spread - high.astype(jnp.float32)).astype(jnp.bfloat16)
    pad = jnp.zeros((tok_dev, -(2 * devices) % LANES), jnp.bfloat16)
    rows = jnp.concatenate([normed, high, low, pad], axis=1)
    moe_out = expert_block(rows, w_gate[0], w_up[0], w_down[0], devices)
    return (ssd_out, moe_out)


def solution(mesh):
    in_specs = (
        P(("group", "wide"), None),
        P(("group", "wide"), None),
        P(("group", "wide"), None),
        P(("group", "wide"), None),
        P(("group", "wide"), None),
        P(),
        P(),
        P(),
        P(),
        P(("group", "wide"), None, None, None),
        P("group"),
        P(("group", "wide"), None),
        P("wide", None),
        P(),
        P(("group", "wide"), None),
        P(("group", "wide"), None),
        P(),
        P("wide", None, None),
        P("wide", None, None),
        P("wide", None, None),
    )
    out_specs = (P(("group", "wide"), None), P(("group", "wide"), None))
    return jax.shard_map(local, mesh=mesh, in_specs=in_specs, out_specs=out_specs, check_vma=False)
```
